32 devices in a mesh: seq: 16 (over z, x, core), head: 2 (over y).
Axes of the slice: x: 2, y: 2, z: 4, core: 2. Of those that a mesh axis runs over, the one named last changes fastest.
Arguments:
- queries: bfloat16 [1, 4096, 16, 128], P(None, 'seq', 'head'), may hold values from -6 to 6
- keys: bfloat16 [1, 4096, 4, 128], P(None, 'seq', 'head'), may hold values from -6 to 6
- values: bfloat16 [1, 4096, 4, 128], P(None, 'seq', 'head'), may hold values from -6 to 6
- norm_gain: float32 [16, 128], P('head'), may hold values from 0.25 to 1.75
- out_grad: bfloat16 [1, 4096, 16, 128], P(None, 'seq', 'head'), may hold values from -6 to 6
- window_reach: int32 [1, 16], P(None, 'seq'), may hold values from 0 to 256
- partner_mask: int32 [1, 16, 3], P(None, 'seq'), may hold values 0 or 1
Outputs:
- normed: bfloat16 [1, 4096, 16, 128], P(None, 'seq', 'head')
- query_grad: bfloat16 [1, 4096, 16, 128], P(None, 'seq', 'head')
- key_gradient: bfloat16 [1, 4096, 4, 128], P(None, 'seq', 'head')
- value_gradient: bfloat16 [1, 4096, 4, 128], P(None, 'seq', 'head')
The draws below stay inside these ranges and needn't reach their ends.
All inputs are finite; a program needn't handle non-finite values. No bound on the sum of `partner_mask` on one device may be relied on, other than what follows from the above.
Results may differ from the reference program's by a relative error of at most 0.029.
Values may be sent and summed in bfloat16 or wider, within the bound.
A program may use at most 64 MiB of HBM per device.

```python
import math
import jax
import jax.numpy as jnp
from jax import lax

QUERY_HEADS = 16
KEY_VALUE_HEADS = 4
HEAD_DIMENSION = 128
BLOCK_TOKENS = 256
SEQUENCE_COUNT = 1
BLOCK_COUNT = 16
SEQUENCE_TOKENS = 4096
QUERIES_PER_KEY = 4
NLEVEL = 3


def draw_queries(key, part):
    noise_random_seed = jax.random.fold_in(key, 5)
    sampled_numbers = jnp.clip(jax.random.normal(noise_random_seed, (SEQUENCE_COUNT, SEQUENCE_TOKENS, QUERY_HEADS, HEAD_DIMENSION), jnp.float32), -6.0, 6.0)
    return sampled_numbers.astype(jnp.bfloat16)


def draw_keys(key, part):
    noise_random_seed = jax.random.fold_in(key, 6)
    sampled_numbers = jnp.clip(jax.random.normal(noise_random_seed, (SEQUENCE_COUNT, SEQUENCE_TOKENS, KEY_VALUE_HEADS, HEAD_DIMENSION), jnp.float32), -6.0, 6.0)
    return sampled_numbers.astype(jnp.bfloat16)


def draw_values(key, part):
    child_seeds = jax.random.split(jax.random.fold_in(key, 7), 3)
    small_noise = jnp.exp(jax.random.uniform(child_seeds[0], (KEY_VALUE_HEADS,), jnp.float32, -0.15, 0.15))
    head_multiplier = 3.0 ** (0.5 * jnp.arange(KEY_VALUE_HEADS, dtype=jnp.float32) / (KEY_VALUE_HEADS - 1)) * small_noise
    row_scale = jnp.exp(jax.random.uniform(child_seeds[1], (SEQUENCE_COUNT, SEQUENCE_TOKENS, 1, 1), jnp.float32, 0.0, 1.1))
    starting_sample = jax.random.normal(child_seeds[2], (SEQUENCE_COUNT, SEQUENCE_TOKENS, KEY_VALUE_HEADS, HEAD_DIMENSION), jnp.float32)
    sampled_numbers = jnp.clip(starting_sample * row_scale * head_multiplier[None, None, :, None], -6.0, 6.0)
    return sampled_numbers.astype(jnp.bfloat16)


def plant(values, own_key, smallest, high):
    place = [jax.random.randint(jax.random.fold_in(own_key, axis), (), 0, length) for axis, length in enumerate(values.shape)]
    main_axis = values.shape.index(max(values.shape))
    beside = place[:main_axis] + [(place[main_axis] + 1) % values.shape[main_axis]] + place[main_axis + 1:]
    return values.at[tuple(place)].set(smallest).at[tuple(beside)].set(high)


def steps_of(rng, dims, pieces, low, top_value):
    loudness = 1.0
    for axis_at, blocks in pieces:
        heights = jax.random.uniform(jax.random.fold_in(jax.random.fold_in(rng, 6), axis_at), (blocks,), jnp.float32, low / len(pieces), top_value / len(pieces))
        loudness = loudness * jnp.repeat(jnp.exp(heights), dims[axis_at] // blocks).reshape((-1,) + (1,) * (len(dims) - 1 - axis_at))
    return loudness


def centred(key, dims, deviation, bound, cuts=(), kind=jnp.bfloat16):
    drawn = jax.random.normal(key, dims, jnp.float32) * deviation
    if len(cuts) > 0:
        drawn = steps_of(key, dims, cuts, -0.22, 0.18) * drawn
    return jnp.clip(drawn, min=-bound, max=bound).astype(kind)


def setup_inputs(seed: int = 0) -> dict:
    key_list = jax.random.split(jax.random.key(seed), 8)
    queries = draw_queries(jax.random.fold_in(key_list[7], 71), 0)
    keys = draw_keys(jax.random.fold_in(key_list[7], 71), 0)
    values = draw_values(jax.random.fold_in(key_list[7], 71), 0)
    norm_gain = jnp.clip(1.0 + 0.15 * jax.random.normal(key_list[3], (QUERY_HEADS, HEAD_DIMENSION), jnp.float32), 0.25, 1.75)
    out_grad = centred(key_list[4], (SEQUENCE_COUNT, SEQUENCE_TOKENS, QUERY_HEADS, HEAD_DIMENSION), 1.0, 6.0, ((1, 16), (2, 2)))
    window_reach = plant(jax.random.randint(key_list[5], (SEQUENCE_COUNT, BLOCK_COUNT), 0, BLOCK_TOKENS + 1), jax.random.fold_in(key_list[5], 1), 0, BLOCK_TOKENS).astype(jnp.int32)
    partner_mask = plant((jax.random.randint(key_list[6], (SEQUENCE_COUNT, BLOCK_COUNT, NLEVEL), 0, 4) < 3).astype(jnp.int32), jax.random.fold_in(key_list[6], 1), 0, 1)
    return dict(queries=queries, keys=keys, values=values, norm_gain=norm_gain, out_grad=out_grad, window_reach=window_reach, partner_mask=partner_mask)


epsilon = 1e-06

def rounded(tensor):
    return lax.optimization_barrier(tensor.astype(jnp.bfloat16)).astype(jnp.float32)

def reference(queries, keys, values, norm_gain, out_grad, window_reach, partner_mask):
    score_scale = 1.0 / math.sqrt(HEAD_DIMENSION)
    offsets = jnp.array([0, 1] + [2 ** level for level in range(1, NLEVEL + 1)], jnp.int32)
    positions = jnp.arange(BLOCK_TOKENS, dtype=jnp.int32)
    blocked_queries = queries.reshape(SEQUENCE_COUNT * BLOCK_COUNT, BLOCK_TOKENS, KEY_VALUE_HEADS, QUERIES_PER_KEY, HEAD_DIMENSION).astype(jnp.float32)
    blocked_keys = keys.reshape(SEQUENCE_COUNT * BLOCK_COUNT, BLOCK_TOKENS, KEY_VALUE_HEADS, HEAD_DIMENSION).astype(jnp.float32)
    blocked_values = values.reshape(SEQUENCE_COUNT * BLOCK_COUNT, BLOCK_TOKENS, KEY_VALUE_HEADS, HEAD_DIMENSION).astype(jnp.float32)

    def pattern(index):
        sequence = index // BLOCK_COUNT
        block_index = index % BLOCK_COUNT
        targets = block_index - offsets
        gathered = (sequence * BLOCK_COUNT + jnp.maximum(targets, 0)).astype(jnp.int32)
        own_mask = positions[None, :] <= positions[:, None]
        window = (positions[None, :] >= BLOCK_TOKENS - window_reach[sequence, block_index]) & (block_index >= 1)
        window = jnp.broadcast_to(window, (BLOCK_TOKENS, BLOCK_TOKENS))
        levels = (partner_mask[sequence, block_index] == 1) & (block_index >= offsets[2:])
        level_masks = jnp.broadcast_to(levels[:, None, None], (NLEVEL, BLOCK_TOKENS, BLOCK_TOKENS))
        allowed = jnp.concatenate([own_mask[None], window[None], level_masks], axis=0)
        return (gathered, allowed.transpose(1, 2, 0))

    def scores_of(index):
        gathered, allowed = pattern(index)
        raw_scores = jnp.einsum('uhgd,tshd->hgust', blocked_queries[index], blocked_keys[gathered]) * score_scale
        return (jnp.where(allowed[None, None], raw_scores, -jnp.inf), gathered)

    def forward(index):
        scores, gathered = scores_of(index)
        row_peak = lax.optimization_barrier(jnp.max(scores, axis=(3, 4)))
        log_total = row_peak + jnp.log(lax.optimization_barrier(jnp.sum(jnp.exp(scores - row_peak[..., None, None]), axis=(3, 4))))
        probabilities = rounded(jnp.exp(scores - log_total[..., None, None]))
        output = jnp.einsum('hgust,tshd->uhgd', probabilities, blocked_values[gathered])
        return (output.astype(jnp.bfloat16), log_total)
    block_ids = jnp.arange(SEQUENCE_COUNT * BLOCK_COUNT, dtype=jnp.int32)
    attn_blocks, log_totals = lax.map(forward, block_ids)
    attn_wide = lax.optimization_barrier(attn_blocks).astype(jnp.float32).reshape(SEQUENCE_COUNT, SEQUENCE_TOKENS, QUERY_HEADS, HEAD_DIMENSION)
    mean_square = lax.optimization_barrier(jnp.mean(attn_wide * attn_wide, axis=(2, 3)))
    inverse = 1.0 / jnp.sqrt(mean_square + epsilon)
    normed = (norm_gain * attn_wide * inverse[..., None, None]).astype(jnp.bfloat16)
    scaled_grad = norm_gain * out_grad.astype(jnp.float32)
    dot_total = lax.optimization_barrier(jnp.sum(scaled_grad * attn_wide, axis=(2, 3)))
    attention_gradient = rounded(scaled_grad * inverse[..., None, None] - attn_wide * (dot_total * inverse ** 3 / (QUERY_HEADS * HEAD_DIMENSION))[..., None, None])
    correction_rows = lax.optimization_barrier(jnp.sum(attention_gradient * attn_wide, axis=-1))
    gradient_blocks = attention_gradient.reshape(SEQUENCE_COUNT * BLOCK_COUNT, BLOCK_TOKENS, KEY_VALUE_HEADS, QUERIES_PER_KEY, HEAD_DIMENSION)
    correction_blocks = correction_rows.reshape(SEQUENCE_COUNT * BLOCK_COUNT, BLOCK_TOKENS, KEY_VALUE_HEADS, QUERIES_PER_KEY)

    def backward(carried, index):
        key_accumulator, value_accumulator = carried
        scores, gathered = scores_of(index)
        weights = jnp.exp(scores - log_totals[index][..., None, None])
        prob_grad = jnp.einsum('uhgd,tshd->hgust', gradient_blocks[index], blocked_values[gathered])
        score_grad = rounded(weights * (prob_grad - correction_blocks[index].transpose(1, 2, 0)[..., None, None]))
        query_part = jnp.einsum('hgust,tshd->uhgd', score_grad, blocked_keys[gathered]) * score_scale
        key_part = jnp.einsum('hgust,uhgd->tshd', score_grad, blocked_queries[index]) * score_scale
        value_part = jnp.einsum('hgust,uhgd->tshd', rounded(weights), gradient_blocks[index])
        return ((key_accumulator.at[gathered].add(key_part), value_accumulator.at[gathered].add(value_part)), query_part.astype(jnp.bfloat16))
    empty_gradients = jnp.zeros((SEQUENCE_COUNT * BLOCK_COUNT, BLOCK_TOKENS, KEY_VALUE_HEADS, HEAD_DIMENSION), jnp.float32)
    (key_accumulator, value_accumulator), query_parts = lax.scan(backward, (empty_gradients, empty_gradients), block_ids)
    query_grad = query_parts.reshape(SEQUENCE_COUNT, SEQUENCE_TOKENS, QUERY_HEADS, HEAD_DIMENSION)
    key_gradient = key_accumulator.astype(jnp.bfloat16).reshape(SEQUENCE_COUNT, SEQUENCE_TOKENS, KEY_VALUE_HEADS, HEAD_DIMENSION)
    value_gradient = value_accumulator.astype(jnp.bfloat16).reshape(SEQUENCE_COUNT, SEQUENCE_TOKENS, KEY_VALUE_HEADS, HEAD_DIMENSION)
    return (normed, query_grad, key_gradient, value_gradient)
```

```python
import math

import jax
import jax.numpy as jnp
from jax import lax
from jax.experimental import pallas as pl
from jax.experimental.pallas import tpu as pltpu
from jax.sharding import PartitionSpec as P

epsilon = 1e-06
MESH = pl.DeviceIdType.MESH
F32 = jnp.float32
BF16 = jnp.bfloat16


def dot_nn(a, b):
    return lax.dot_general(a, b, (((1,), (0,)), ((), ())), preferred_element_type=F32)


def dot_nt(a, b):
    return lax.dot_general(a, b, (((1,), (1,)), ((), ())), preferred_element_type=F32)


def make_kernel(n, heads, levels, group, kv_heads, rows, size):
    local_heads = group * kv_heads
    scale = 1.0 / math.sqrt(size)
    c = scale * math.log2(math.e)
    features = float(local_heads * heads * size)
    slots = levels + 1
    neg, pos = -float("inf"), float("inf")

    def distance(i):
        return 2**i

    def step(i):
        return 2**i if i <= 2 else 2 ** (i - 1)

    steps = sorted({step(i) for i in range(slots)})

    def kernel(
        reach_ref, partner_ref, kv_ref, q_ref, og_ref, gain_ref,
        normed_ref, dq_ref, dk_ref, dv_ref,
        kvr, gsend, grecv, gown, wide, q_scr, sg, probs, m_scr, l_scr, mblk, acc, attn, da, delta,
        stat_own, stat_in,
        fsend, frecv, bsend, brecv, ssend, srecv,
    ):
        me = lax.axis_index("seq")
        hd = lax.axis_index("head")

        barrier = pltpu.get_barrier_semaphore()
        count = jnp.int32(heads - 1)
        for d in steps:
            @pl.when(me + d < n)
            def _():
                pl.semaphore_signal(barrier, inc=1, device_id=(me + d, hd), device_id_type=MESH)

            @pl.when(me >= d)
            def _():
                pl.semaphore_signal(barrier, inc=1, device_id=(me - d, hd), device_id_type=MESH)

            count = count + jnp.where(me + d < n, 1, 0) + jnp.where(me >= d, 1, 0)
        for o in range(1, heads):
            pl.semaphore_signal(
                barrier, inc=1, device_id=(me, lax.rem(hd + o, heads)), device_id_type=MESH
            )
        pl.semaphore_wait(barrier, count)

        def forward_copy(i, g):
            source = kv_ref.at[g] if i <= 2 else kvr.at[i - 1, g]
            return pltpu.make_async_remote_copy(
                src_ref=source, dst_ref=kvr.at[i, g],
                send_sem=fsend.at[i, g], recv_sem=frecv.at[i, g],
                device_id=(me + step(i), hd), device_id_type=MESH,
            )

        def backward_copy(i, g):
            return pltpu.make_async_remote_copy(
                src_ref=gsend.at[i, g], dst_ref=grecv.at[i, g],
                send_sem=bsend.at[i, g], recv_sem=brecv.at[i, g],
                device_id=(me - step(i), hd), device_id_type=MESH,
            )

        def sends(i):
            if i <= 2:
                return me + step(i) < n
            return (me + step(i) < n) & (me >= step(i))

        def has(i):
            return me >= distance(i)

        def gets_back(i):
            return (me + step(i) < n) & (me + step(i) >= distance(i))

        for i in [i for i in (2, 0, 1) if i < slots]:
            @pl.when(sends(i))
            def _():
                for g in range(kv_heads):
                    forward_copy(i, g).start()

        wide[...] = q_ref[...].astype(F32).reshape(rows * local_heads, size)
        for h in range(local_heads):
            q_scr[h] = wide[pl.ds(h, rows, stride=local_heads), :].astype(BF16)

        key_pos = lax.broadcasted_iota(jnp.int32, (rows, rows), 0)
        query_pos = lax.broadcasted_iota(jnp.int32, (rows, rows), 1)

        def forward_block(pi, g, kv):
            key, value = kv[0], kv[1]
            value_t = value.T
            for k in range(group):
                h = g * group + k
                s = dot_nt(key, q_scr[h])
                if pi == 0:
                    s = jnp.where(key_pos <= query_pos, s, neg)
                elif pi == 1:
                    s = jnp.where(key_pos >= rows - reach_ref[0, 0], s, neg)
                top = jnp.max(s, axis=0, keepdims=True)
                if pi >= 2:
                    on = partner_ref[0, pi - 2] == 1
                    top = top + jnp.where(on, 0.0, neg)
                if pi == 0:
                    m = top
                else:
                    old = m_scr[h]
                    m = jnp.maximum(old, top)
                shift = m * c
                if pi >= 2:
                    shift = shift + jnp.where(on, 0.0, pos)
                p = jnp.exp2(s * c - shift)
                total = jnp.sum(p, axis=0, keepdims=True)
                pb = p.astype(BF16)
                probs[pi, h] = pb
                part = dot_nn(value_t, pb)
                if pi == 0:
                    l_scr[h] = total
                    acc[h] = part
                else:
                    alpha = jnp.exp2((old - m) * c)
                    l_scr[h] = l_scr[h] * alpha + total
                    acc[h] = acc[h] * alpha + part
                m_scr[h] = m
                mblk[pi, h] = m

        @pl.loop(0, kv_heads)
        def _(g):
            forward_block(0, g, kv_ref.at[g])

        wide[...] = og_ref[...].astype(F32).reshape(rows * local_heads, size)
        for h in range(local_heads):
            piece = wide[pl.ds(h, rows, stride=local_heads), :] * gain_ref[h : h + 1, :]
            sg[h] = piece.T

        for i in range(slots):
            @pl.when(has(i))
            def _():
                @pl.loop(0, kv_heads)
                def _(g):
                    forward_copy(i, g).wait_recv()
                    if i >= 2 and i + 1 < slots:
                        @pl.when(sends(i + 1))
                        def _():
                            forward_copy(i + 1, g).start()
                    forward_block(i + 1, g, kvr.at[i, g])

        def first_sums(h, carry):
            square, dot = carry
            a = (acc[h] * (1.0 / l_scr[h])).astype(BF16)
            attn[h] = a
            af = a.astype(F32)
            return (
                square + jnp.sum(af * af, axis=0, keepdims=True),
                dot + jnp.sum(sg[h] * af, axis=0, keepdims=True),
            )

        zero = jnp.zeros((1, rows), F32)
        square, dot = lax.fori_loop(0, local_heads, first_sums, (zero, zero))
        stat_own[...] = jnp.zeros((8, rows), F32)
        stat_own[0:1, :] = square
        stat_own[1:2, :] = dot

        def stat_copy(o):
            return pltpu.make_async_remote_copy(
                src_ref=stat_own, dst_ref=stat_in.at[o - 1],
                send_sem=ssend.at[o - 1], recv_sem=srecv.at[o - 1],
                device_id=(me, lax.rem(hd + o, heads)), device_id_type=MESH,
            )

        for o in range(1, heads):
            stat_copy(o).start()
        for o in range(1, heads):
            stat_copy(o).wait()
            square = square + stat_in[o - 1, 0:1, :]
            dot = dot + stat_in[o - 1, 1:2, :]
        inverse = lax.rsqrt(square / features + epsilon)
        pull = dot * (inverse * inverse * inverse) / features

        @pl.loop(0, local_heads)
        def _(h):
            af = attn[h].astype(F32)
            grad = (sg[h] * inverse - af * pull).astype(BF16)
            da[h] = grad
            delta[h] = jnp.sum(grad.astype(F32) * af, axis=0, keepdims=True)
            acc[h] = jnp.zeros((size, rows), F32)

        def backward_block(pi, g, kv):
            key, value = kv[0], kv[1]
            key_t = key.T
            dk = jnp.zeros((rows, size), F32)
            dv = jnp.zeros((rows, size), F32)
            for k in range(group):
                h = g * group + k
                r = jnp.exp2((mblk[pi, h] - m_scr[h]) * c) / l_scr[h]
                dar = (da[h].astype(F32) * r).astype(BF16)
                dp = dot_nn(value, dar)
                pb = probs[pi, h]
                ds = (pb.astype(F32) * (dp - delta[h] * r)).astype(BF16)
                acc[h] += dot_nn(key_t, ds)
                dk = dk + dot_nn(ds, q_scr[h])
                dv = dv + dot_nt(pb, dar)
            return dk, dv

        for i in [*range(slots - 1, 1, -1), *range(min(slots, 2) - 1, -1, -1)]:
            @pl.when(has(i))
            def _():
                @pl.loop(0, kv_heads)
                def _(g):
                    dk, dv = backward_block(i + 1, g, kvr.at[i, g])
                    gown[g, 0] = dk
                    gown[g, 1] = dv
                    if i >= 2 and i + 1 < slots:
                        @pl.when(gets_back(i + 1))
                        def _():
                            backward_copy(i + 1, g).wait_recv()
                            gown[g] += grecv[i + 1, g].astype(F32)
                    gsend[i, g] = gown[g].astype(BF16)
                    backward_copy(i, g).start()

        @pl.loop(0, kv_heads)
        def _(g):
            dk, dv = backward_block(0, g, kv_ref.at[g])
            gown[g, 0] = dk
            gown[g, 1] = dv

        for h in range(local_heads):
            dq_ref[:, h * size : (h + 1) * size] = (acc[h] * scale).T.astype(BF16)
            tile = (attn[h].astype(F32) * inverse).T * gain_ref[h : h + 1, :]
            normed_ref[:, h * size : (h + 1) * size] = tile.astype(BF16)

        for i in [i for i in (0, 1, 2) if i < slots]:
            @pl.when(gets_back(i))
            def _():
                for g in range(kv_heads):
                    backward_copy(i, g).wait_recv()
                    gown[g] += grecv[i, g].astype(F32)
        for g in range(kv_heads):
            dk_ref[:, g * size : (g + 1) * size] = (gown[g, 0] * scale).astype(BF16)
            dv_ref[:, g * size : (g + 1) * size] = gown[g, 1].astype(BF16)

        for i in range(slots):
            @pl.when(sends(i))
            def _():
                for g in range(kv_heads):
                    forward_copy(i, g).wait_send()

            @pl.when(has(i))
            def _():
                for g in range(kv_heads):
                    backward_copy(i, g).wait_send()

    return kernel


def solution(mesh):
    n, heads = mesh.shape["seq"], mesh.shape["head"]
    levels = len([j for j in range(1, 11) if 2 ** (j + 1) <= n])

    def per_device(queries, keys, values, norm_gain, out_grad, window_reach, partner_mask):
        _, rows, local_heads, size = queries.shape
        kv_heads = keys.shape[2]
        group = local_heads // kv_heads
        slots = levels + 1
        k2 = keys[0].transpose(1, 0, 2)
        v2 = values[0].transpose(1, 0, 2)
        kv = jnp.stack([k2, v2], axis=1)
        vmem = pl.BlockSpec(memory_space=pltpu.VMEM)
        smem = pl.BlockSpec(memory_space=pltpu.SMEM)
        dma = pltpu.SemaphoreType.DMA
        wide_shape = (rows, local_heads * size)
        thin_shape = (rows, kv_heads * size)
        normed, dq, dk, dv = pl.pallas_call(
            make_kernel(n, heads, levels, group, kv_heads, rows, size),
            out_shape=[
                jax.ShapeDtypeStruct(wide_shape, BF16),
                jax.ShapeDtypeStruct(wide_shape, BF16),
                jax.ShapeDtypeStruct(thin_shape, BF16),
                jax.ShapeDtypeStruct(thin_shape, BF16),
            ],
            in_specs=[smem, smem, vmem, vmem, vmem, vmem],
            out_specs=[vmem] * 4,
            scratch_shapes=[
                pltpu.VMEM((slots, kv_heads, 2, rows, size), BF16),
                pltpu.VMEM((slots, kv_heads, 2, rows, size), BF16),
                pltpu.VMEM((slots, kv_heads, 2, rows, size), BF16),
                pltpu.VMEM((kv_heads, 2, rows, size), F32),
                pltpu.VMEM((rows * local_heads, size), F32),
                pltpu.VMEM((local_heads, rows, size), BF16),
                pltpu.VMEM((local_heads, size, rows), F32),
                pltpu.VMEM((slots + 1, local_heads, rows, rows), BF16),
                pltpu.VMEM((local_heads, 1, rows), F32),
                pltpu.VMEM((local_heads, 1, rows), F32),
                pltpu.VMEM((slots + 1, local_heads, 1, rows), F32),
                pltpu.VMEM((local_heads, size, rows), F32),
                pltpu.VMEM((local_heads, size, rows), BF16),
                pltpu.VMEM((local_heads, size, rows), BF16),
                pltpu.VMEM((local_heads, 1, rows), F32),
                pltpu.VMEM((8, rows), F32),
                pltpu.VMEM((max(heads - 1, 1), 8, rows), F32),
                dma((slots, kv_heads)), dma((slots, kv_heads)),
                dma((slots, kv_heads)), dma((slots, kv_heads)),
                dma((max(heads - 1, 1),)), dma((max(heads - 1, 1),)),
            ],
            compiler_params=pltpu.CompilerParams(
                collective_id=0, has_side_effects=True, vmem_limit_bytes=48 * 1024 * 1024
            ),
        )(
            window_reach, partner_mask[0], kv, queries[0], out_grad[0], norm_gain
        )
        full = (1, rows, local_heads, size)
        thin = (1, rows, kv_heads, size)
        return normed.reshape(full), dq.reshape(full), dk.reshape(thin), dv.reshape(thin)

    wide_spec = P(None, "seq", "head", None)
    return jax.shard_map(
        per_device,
        mesh=mesh,
        in_specs=(
            wide_spec, wide_spec, wide_spec, P("head", None), wide_spec,
            P(None, "seq"), P(None, "seq", None),
        ),
        out_specs=(wide_spec,) * 4,
        check_vma=False,
    )
```

```python
import math

import jax
import jax.numpy as jnp
from jax import lax
from jax.experimental import pallas as pl
from jax.experimental.pallas import tpu as pltpu
from jax.sharding import PartitionSpec as P

epsilon = 1e-06
MESH = pl.DeviceIdType.MESH
F32 = jnp.float32
BF16 = jnp.bfloat16


def dot_nn(a, b):
    return lax.dot_general(a, b, (((1,), (0,)), ((), ())), preferred_element_type=F32)


def dot_nt(a, b):
    return lax.dot_general(a, b, (((1,), (1,)), ((), ())), preferred_element_type=F32)


def make_kernel(n, heads, levels, group, kv_heads, rows, size):
    local_heads = group * kv_heads
    scale = 1.0 / math.sqrt(size)
    c = scale * math.log2(math.e)
    features = float(local_heads * heads * size)
    slots = levels + 1
    neg, pos = -float("inf"), float("inf")

    def distance(i):
        return 2**i

    def step(i):
        return 2**i if i <= 2 else 2 ** (i - 1)

    steps = sorted({step(i) for i in range(slots)})

    def kernel(
        reach_ref, partner_ref, kv_ref, q_ref, og_ref, gain_ref,
        normed_ref, dq_ref, dk_ref, dv_ref,
        kvr, gsend, grecv, gown, wide, q_scr, sg, probs, m_scr, l_scr, mblk, acc, attn, da, delta,
        stat_own, stat_in,
        fsend, frecv, bsend, brecv, ssend, srecv,
    ):
        me = lax.axis_index("seq")
        hd = lax.axis_index("head")

        barrier = pltpu.get_barrier_semaphore()
        count = jnp.int32(heads - 1)
        for d in steps:
            @pl.when(me + d < n)
            def _():
                pl.semaphore_signal(barrier, inc=1, device_id=(me + d, hd), device_id_type=MESH)

            @pl.when(me >= d)
            def _():
                pl.semaphore_signal(barrier, inc=1, device_id=(me - d, hd), device_id_type=MESH)

            count = count + jnp.where(me + d < n, 1, 0) + jnp.where(me >= d, 1, 0)
        for o in range(1, heads):
            pl.semaphore_signal(
                barrier, inc=1, device_id=(me, lax.rem(hd + o, heads)), device_id_type=MESH
            )
        pl.semaphore_wait(barrier, count)

        even = lax.rem(me, 2) == 0
        low = lax.rem(me, 4) < 2

        def has(i):
            return me >= distance(i)

        def gets_back(i):
            return (me + step(i) < n) & (me >= step(i))

        routes = {
            "own2": (me + 4 < n, None, 2, me + 4),
            "own1": (low, None, 1, me + 2),
            "own0": (even, None, 0, me + 1),
            "pass1": (jnp.logical_not(low) & has(2), 2, 1, me - 2),
            "pass0": (jnp.logical_not(even) & has(1), 1, 0, me - 1),
        }
        for i in range(3, slots):
            routes[i] = ((me + step(i) < n) & has(i - 1), i - 1, i, me + step(i))
        order = {name: at for at, name in enumerate(routes)}

        def route_copy(name, g):
            _, source, slot, target = routes[name]
            return pltpu.make_async_remote_copy(
                src_ref=kv_ref.at[g] if source is None else kvr.at[source, g],
                dst_ref=kvr.at[slot, g],
                send_sem=fsend.at[order[name], g], recv_sem=frecv.at[slot, g],
                device_id=(target, hd), device_id_type=MESH,
            )

        def send(name, g):
            @pl.when(routes[name][0])
            def _():
                route_copy(name, g).start()

        def arrived(i, g):
            route_copy({0: "own0", 1: "own1", 2: "own2"}.get(i, i), g).wait_recv()

        def backward_copy(i, g):
            if i == 0:
                target = jnp.where(even, me + 1, me - 1)
            elif i == 1:
                target = jnp.where(low, me + 2, me - 2)
            else:
                target = me - step(i)
            return pltpu.make_async_remote_copy(
                src_ref=gsend.at[i, g], dst_ref=grecv.at[i, g],
                send_sem=bsend.at[i, g], recv_sem=brecv.at[i, g],
                device_id=(target, hd), device_id_type=MESH,
            )

        for name in ("own2", "own1", "own0"):
            for g in range(kv_heads):
                send(name, g)

        wide[...] = q_ref[...].astype(F32).reshape(rows * local_heads, size)
        for h in range(local_heads):
            q_scr[h] = wide[pl.ds(h, rows, stride=local_heads), :].astype(BF16)

        key_pos = lax.broadcasted_iota(jnp.int32, (rows, rows), 0)
        query_pos = lax.broadcasted_iota(jnp.int32, (rows, rows), 1)

        def forward_block(pi, g, kv):
            key, value = kv[0], kv[1]
            value_t = value.T
            for k in range(group):
                h = g * group + k
                s = dot_nt(key, q_scr[h])
                if pi == 0:
                    s = jnp.where(key_pos <= query_pos, s, neg)
                elif pi == 1:
                    s = jnp.where(key_pos >= rows - reach_ref[0, 0], s, neg)
                top = jnp.max(s, axis=0, keepdims=True)
                if pi >= 2:
                    on = partner_ref[0, pi - 2] == 1
                    top = top + jnp.where(on, 0.0, neg)
                if pi == 0:
                    m = top
                else:
                    old = m_scr[h]
                    m = jnp.maximum(old, top)
                shift = m * c
                if pi >= 2:
                    shift = shift + jnp.where(on, 0.0, pos)
                p = jnp.exp2(s * c - shift)
                total = jnp.sum(p, axis=0, keepdims=True)
                pb = p.astype(BF16)
                probs[pi, h] = pb
                part = dot_nn(value_t, pb)
                if pi == 0:
                    l_scr[h] = total
                    acc[h] = part
                else:
                    alpha = jnp.exp2((old - m) * c)
                    l_scr[h] = l_scr[h] * alpha + total
                    acc[h] = acc[h] * alpha + part
                m_scr[h] = m
                mblk[pi, h] = m

        @pl.loop(0, kv_heads)
        def _(g):
            forward_block(0, g, kv_ref.at[g])

            @pl.when(has(2))
            def _():
                arrived(2, g)
                if slots > 3:
                    send(3, g)
                send("pass1", g)

        wide[...] = og_ref[...].astype(F32).reshape(rows * local_heads, size)
        for h in range(local_heads):
            piece = wide[pl.ds(h, rows, stride=local_heads), :] * gain_ref[h : h + 1, :]
            sg[h] = piece.T

        for i in (2, 1, 0, *range(3, slots)):
            @pl.when(has(i))
            def _():
                if i == 1:
                    for g in range(kv_heads):
                        arrived(1, g)
                        send("pass0", g)

                @pl.loop(0, kv_heads)
                def _(g):
                    if i == 0 or i >= 3:
                        arrived(i, g)
                    if i >= 3 and i + 1 < slots:
                        send(i + 1, g)
                    forward_block(i + 1, g, kvr.at[i, g])

        def first_sums(h, carry):
            square, dot = carry
            a = (acc[h] * (1.0 / l_scr[h])).astype(BF16)
            attn[h] = a
            af = a.astype(F32)
            return (
                square + jnp.sum(af * af, axis=0, keepdims=True),
                dot + jnp.sum(sg[h] * af, axis=0, keepdims=True),
            )

        zero = jnp.zeros((1, rows), F32)
        square, dot = lax.fori_loop(0, local_heads, first_sums, (zero, zero))
        stat_own[...] = jnp.zeros((8, rows), F32)
        stat_own[0:1, :] = square
        stat_own[1:2, :] = dot

        def stat_copy(o):
            return pltpu.make_async_remote_copy(
                src_ref=stat_own, dst_ref=stat_in.at[o - 1],
                send_sem=ssend.at[o - 1], recv_sem=srecv.at[o - 1],
                device_id=(me, lax.rem(hd + o, heads)), device_id_type=MESH,
            )

        for o in range(1, heads):
            stat_copy(o).start()
        for o in range(1, heads):
            stat_copy(o).wait()
            square = square + stat_in[o - 1, 0:1, :]
            dot = dot + stat_in[o - 1, 1:2, :]
        inverse = lax.rsqrt(square / features + epsilon)
        pull = dot * (inverse * inverse * inverse) / features

        @pl.loop(0, local_heads)
        def _(h):
            af = attn[h].astype(F32)
            grad = (sg[h] * inverse - af * pull).astype(BF16)
            da[h] = grad
            delta[h] = jnp.sum(grad.astype(F32) * af, axis=0, keepdims=True)
            acc[h] = jnp.zeros((size, rows), F32)

        def backward_block(pi, g, kv):
            key, value = kv[0], kv[1]
            key_t = key.T
            dk = jnp.zeros((rows, size), F32)
            dv = jnp.zeros((rows, size), F32)
            for k in range(group):
                h = g * group + k
                r = jnp.exp2((mblk[pi, h] - m_scr[h]) * c) / l_scr[h]
                dar = (da[h].astype(F32) * r).astype(BF16)
                dp = dot_nn(value, dar)
                pb = probs[pi, h]
                ds = (pb.astype(F32) * (dp - delta[h] * r)).astype(BF16)
                acc[h] += dot_nn(key_t, ds)
                dk = dk + dot_nn(ds, q_scr[h])
                dv = dv + dot_nt(pb, dar)
            return dk, dv

        for i in (*range(slots - 1, 2, -1), 0, 1, 2):
            feeds = []
            if i == 1:
                feeds.append((0, jnp.logical_not(even)))
            if i == 2:
                feeds.append((1, jnp.logical_not(low) & (me >= 6)))
            if i >= 2 and i + 1 < slots:
                feeds.append((i + 1, gets_back(i + 1)))

            @pl.when(has(i))
            def _():
                @pl.loop(0, kv_heads)
                def _(g):
                    dk, dv = backward_block(i + 1, g, kvr.at[i, g])
                    gown[g, 0] = dk
                    gown[g, 1] = dv
                    for feed, cond in feeds:
                        @pl.when(cond)
                        def _():
                            backward_copy(feed, g).wait_recv()
                            gown[g] += grecv[feed, g].astype(F32)
                    gsend[i, g] = gown[g].astype(BF16)
                    backward_copy(i, g).start()

        @pl.loop(0, kv_heads)
        def _(g):
            dk, dv = backward_block(0, g, kv_ref.at[g])
            gown[g, 0] = dk
            gown[g, 1] = dv

        for h in range(local_heads):
            dq_ref[:, h * size : (h + 1) * size] = (acc[h] * scale).T.astype(BF16)
            tile = (attn[h].astype(F32) * inverse).T * gain_ref[h : h + 1, :]
            normed_ref[:, h * size : (h + 1) * size] = tile.astype(BF16)

        for i, cond in ((0, even), (1, low), (2, me + 4 < n)):
            @pl.when(cond)
            def _():
                for g in range(kv_heads):
                    backward_copy(i, g).wait_recv()
                    gown[g] += grecv[i, g].astype(F32)
        for g in range(kv_heads):
            dk_ref[:, g * size : (g + 1) * size] = (gown[g, 0] * scale).astype(BF16)
            dv_ref[:, g * size : (g + 1) * size] = gown[g, 1].astype(BF16)

        for name in routes:
            @pl.when(routes[name][0])
            def _():
                for g in range(kv_heads):
                    route_copy(name, g).wait_send()

        for i in range(slots):
            @pl.when(has(i))
            def _():
                for g in range(kv_heads):
                    backward_copy(i, g).wait_send()

    return kernel


def solution(mesh):
    n, heads = mesh.shape["seq"], mesh.shape["head"]
    levels = len([j for j in range(1, 11) if 2 ** (j + 1) <= n])

    def per_device(queries, keys, values, norm_gain, out_grad, window_reach, partner_mask):
        _, rows, local_heads, size = queries.shape
        kv_heads = keys.shape[2]
        group = local_heads // kv_heads
        slots = levels + 1
        k2 = keys[0].transpose(1, 0, 2)
        v2 = values[0].transpose(1, 0, 2)
        kv = jnp.stack([k2, v2], axis=1)
        vmem = pl.BlockSpec(memory_space=pltpu.VMEM)
        smem = pl.BlockSpec(memory_space=pltpu.SMEM)
        dma = pltpu.SemaphoreType.DMA
        wide_shape = (rows, local_heads * size)
        thin_shape = (rows, kv_heads * size)
        normed, dq, dk, dv = pl.pallas_call(
            make_kernel(n, heads, levels, group, kv_heads, rows, size),
            out_shape=[
                jax.ShapeDtypeStruct(wide_shape, BF16),
                jax.ShapeDtypeStruct(wide_shape, BF16),
                jax.ShapeDtypeStruct(thin_shape, BF16),
                jax.ShapeDtypeStruct(thin_shape, BF16),
            ],
            in_specs=[smem, smem, vmem, vmem, vmem, vmem],
            out_specs=[vmem] * 4,
            scratch_shapes=[
                pltpu.VMEM((slots, kv_heads, 2, rows, size), BF16),
                pltpu.VMEM((slots, kv_heads, 2, rows, size), BF16),
                pltpu.VMEM((slots, kv_heads, 2, rows, size), BF16),
                pltpu.VMEM((kv_heads, 2, rows, size), F32),
                pltpu.VMEM((rows * local_heads, size), F32),
                pltpu.VMEM((local_heads, rows, size), BF16),
                pltpu.VMEM((local_heads, size, rows), F32),
                pltpu.VMEM((slots + 1, local_heads, rows, rows), BF16),
                pltpu.VMEM((local_heads, 1, rows), F32),
                pltpu.VMEM((local_heads, 1, rows), F32),
                pltpu.VMEM((slots + 1, local_heads, 1, rows), F32),
                pltpu.VMEM((local_heads, size, rows), F32),
                pltpu.VMEM((local_heads, size, rows), BF16),
                pltpu.VMEM((local_heads, size, rows), BF16),
                pltpu.VMEM((local_heads, 1, rows), F32),
                pltpu.VMEM((8, rows), F32),
                pltpu.VMEM((max(heads - 1, 1), 8, rows), F32),
                dma((slots + 2, kv_heads)), dma((slots, kv_heads)),
                dma((slots, kv_heads)), dma((slots, kv_heads)),
                dma((max(heads - 1, 1),)), dma((max(heads - 1, 1),)),
            ],
            compiler_params=pltpu.CompilerParams(
                collective_id=0, has_side_effects=True, vmem_limit_bytes=48 * 1024 * 1024
            ),
        )(
            window_reach, partner_mask[0], kv, queries[0], out_grad[0], norm_gain
        )
        full = (1, rows, local_heads, size)
        thin = (1, rows, kv_heads, size)
        return normed.reshape(full), dq.reshape(full), dk.reshape(thin), dv.reshape(thin)

    wide_spec = P(None, "seq", "head", None)
    return jax.shard_map(
        per_device,
        mesh=mesh,
        in_specs=(
            wide_spec, wide_spec, wide_spec, P("head", None), wide_spec,
            P(None, "seq"), P(None, "seq", None),
        ),
        out_specs=(wide_spec,) * 4,
        check_vma=False,
    )
```
